32 devices in a mesh: parts: 2 (over x), ctx: 16 (over z, y, core).
Axes of the slice: x: 2, y: 2, z: 4, core: 2. Of those that a mesh axis runs over, the one named last changes fastest.
Arguments:
- query_proj: bfloat16 [4096, 4096], P(('parts', 'ctx')), parts along dimension 0, may hold values from -6 to 6
- key_proj: bfloat16 [4096, 4096], P(('parts', 'ctx')), parts along dimension 0, may hold values from -6 to 6
- value_proj: bfloat16 [4096, 4096], P(('parts', 'ctx')), parts along dimension 0, may hold values from -6 to 6
- cotangent: bfloat16 [4096, 2048], P(('parts', 'ctx')), parts along dimension 0, may hold values from -6 to 6
- out_weight: bfloat16 [4096, 2048], P('ctx'), may hold values from -0.125 to 0.125
- filters: float32 [256, 2048], P('ctx'), may hold values from -1.2 to 1.2
Outputs:
- query_grad: float32 [4096, 4096], P(('parts', 'ctx')), parts along dimension 0
- key_grad: float32 [4096, 4096], P(('parts', 'ctx')), parts along dimension 0
- value_grad: float32 [4096, 4096], P(('parts', 'ctx')), parts along dimension 0
- filter_grad: float32 [512, 2048], P(('parts', 'ctx')), parts along dimension 0
The draws below stay inside these ranges and needn't reach their ends.
There are 2 independent parts, one for each index of `parts`. The reference program is written for one: setup_inputs(seed, part) draws one part's arguments, and reference() takes and returns one part's arrays. A program takes and returns all parts, laid end to end along the dimension named above; an argument that names none is the same for every part. Nothing has to cross between parts.
All inputs are finite; a program needn't handle non-finite values.
Results may differ from the reference program's by a relative error of at most 0.005.
Values may be sent and summed in bfloat16 or wider, within the bound.
A program may use at most 192 MiB of HBM per device.

```python
import math
import jax
import jax.numpy as jnp
from jax import lax

D = 4096
DOUT = 2048
GROUP = 16
SEQ = 2048
GROUPS = 256


def draw_filters(key, part):
    key_tau, key_noise = jax.random.split(key)
    time_index = jnp.arange(SEQ, dtype=jnp.float32)[None, :]
    log_tau = jax.random.uniform(key_tau, (GROUPS, 1), jnp.float32, math.log(24.0), math.log(4.0 * SEQ))
    noise_field = jax.random.truncated_normal(key_noise, -4.0, 4.0, (GROUPS, SEQ), jnp.float32)
    decay_time = jnp.exp(log_tau)
    energy = 0.5 * decay_time * (1.0 - jnp.exp(-2.0 * SEQ / decay_time)) + 0.5
    return noise_field * jnp.exp(-time_index / decay_time) / jnp.sqrt(energy)


def steps_of(rng, dims, shards, low, high):
    loudness = 1.0
    for axis_at, shards_of in shards:
        steps = jax.random.uniform(jax.random.fold_in(jax.random.fold_in(rng, 6), axis_at), (shards_of,), jnp.float32, low / len(shards), high / len(shards))
        loudness = loudness * jnp.repeat(jnp.exp(steps), dims[axis_at] // shards_of).reshape((-1,) + (1,) * (len(dims) - 1 - axis_at))
    return loudness


def gaussian(key, dims, width, limit, pieces=(), kind=jnp.bfloat16):
    factor_of = steps_of(key, dims, pieces, -0.22, 0.18) if pieces else 1.0
    values = jax.random.normal(key, dims, jnp.float32) * width * factor_of
    return jnp.minimum(jnp.maximum(values, -limit), limit).astype(kind)


def setup_inputs(seed: int = 0, part: int = 0) -> dict:
    key_list = jax.random.split(jax.random.key(seed), 7)
    part_keys = jax.random.split(jax.random.fold_in(key_list[6], part), 7)
    query_proj = gaussian(part_keys[0], (SEQ, D), 1.0, 6.0, ((0, 16),))
    key_proj = gaussian(part_keys[1], (SEQ, D), 1.0, 6.0, ((0, 16),))
    value_proj = gaussian(part_keys[2], (SEQ, D), 1.0, 6.0, ((0, 16),))
    cotangent = gaussian(part_keys[3], (SEQ, DOUT), 1.0, 6.0, ((0, 16),))
    out_weight = gaussian(key_list[4], (D, DOUT), DOUT ** -0.5, 0.125, ((0, 16),))
    filters = draw_filters(jax.random.fold_in(key_list[6], 71), part)
    return {"query_proj": query_proj, "key_proj": key_proj, "value_proj": value_proj, "cotangent": cotangent, "out_weight": out_weight, "filters": filters}


def rounded_product(left, right):
    product = (left.astype(jnp.float32) * right.astype(jnp.float32)).astype(jnp.bfloat16)
    return lax.optimization_barrier(product).astype(jnp.float32)


def reference(query_proj, key_proj, value_proj, cotangent, out_weight, filters):
    grad_gated = jnp.dot(cotangent, out_weight.T, preferred_element_type=jnp.float32).astype(jnp.bfloat16)
    fft_len = 2 * SEQ
    grad_scale = (GROUP * SEQ) ** -0.5

    def regroup(array):
        return array.reshape(SEQ, GROUPS, GROUP).transpose(1, 0, 2)

    def one_group(inputs):
        query_block, key_block, value_block, grad_block, filter_row = inputs
        mixed = rounded_product(key_block, value_block)
        gated = rounded_product(query_block, grad_block)
        mixed_spec = jnp.fft.rfft(mixed, n=fft_len, axis=0)
        gated_spec = jnp.fft.rfft(gated, n=fft_len, axis=0)
        filter_spec = jnp.fft.rfft(filter_row, n=fft_len)[:, None]
        conv_out = jnp.fft.irfft(filter_spec * mixed_spec, n=fft_len, axis=0)[:SEQ]
        mixed_grad = jnp.fft.irfft(jnp.conj(filter_spec) * gated_spec, n=fft_len, axis=0)[:SEQ]
        lag_spec = jnp.sum(jnp.conj(mixed_spec) * gated_spec, axis=1)
        lag_sum = jnp.fft.irfft(lag_spec, n=fft_len)[:SEQ]
        query_part = grad_block.astype(jnp.float32) * conv_out
        key_part = mixed_grad * value_block.astype(jnp.float32)
        value_part = mixed_grad * key_block.astype(jnp.float32)
        return query_part, key_part, value_part, lag_sum * grad_scale

    query_all, key_all, value_all, filter_grad = lax.map(
        one_group, (regroup(query_proj), regroup(key_proj), regroup(value_proj), regroup(grad_gated), filters))

    def ungroup(array):
        return array.transpose(1, 0, 2).reshape(SEQ, D)

    return ungroup(query_all), ungroup(key_all), ungroup(value_all), filter_grad
```

```python
import math

import jax
import jax.numpy as jnp
from jax import lax
from jax.experimental import pallas as pl
from jax.experimental.pallas import tpu as pltpu
from jax.sharding import PartitionSpec as P

inner_len = 128


def dft_pair(size_count):
    index_row = jnp.arange(size_count, dtype=jnp.int32)
    phase = (index_row[:, None] * index_row[None, :] % size_count).astype(jnp.float32) * (
        -2.0 * math.pi / size_count
    )
    return (jnp.cos(phase), jnp.sin(phase))


def twist(spectrum, sign):
    outer_len = spectrum.shape[1]
    total = outer_len * inner_len
    outer_index = jnp.arange(outer_len, dtype=jnp.int32)[:, None, None]
    inner_index = jnp.arange(inner_len, dtype=jnp.int32)[None, None, :]
    phase = (outer_index * inner_index % total).astype(jnp.float32) * (-2.0 * math.pi / total)
    tw_real = jnp.cos(phase)
    tw_imag = jnp.sin(phase) * sign
    real_part = spectrum[0] * tw_real - spectrum[1] * tw_imag
    imag_part = spectrum[0] * tw_imag + spectrum[1] * tw_real
    return jnp.stack([real_part, imag_part])


def last_matrix(sign):
    last_real, last_imag = dft_pair(inner_len)
    last_imag = last_imag * sign
    return jnp.stack([jnp.stack([last_real, -last_imag]), jnp.stack([last_imag, last_real])])


def apply_last(spectrum, sign):
    return jnp.einsum(
        "qzcn,pqkn->pzck", spectrum, last_matrix(sign), precision=lax.Precision.HIGHEST
    )


def forward_spectrum(signal):
    half_rows = signal.shape[0]
    outer_len = 2 * half_rows
    lead_real, lead_imag = dft_pair(outer_len)
    lead = jnp.stack([lead_real[:, :half_rows], lead_imag[:, :half_rows]])
    spectrum = jnp.einsum("pzn,ncm->pzcm", lead, signal, precision=lax.Precision.HIGHEST)
    return apply_last(twist(spectrum, 1.0), 1.0)


def inverse_spectrum(spectrum, want_imag):
    outer_len = spectrum.shape[1]
    half_rows = outer_len // 2
    spectrum = twist(apply_last(spectrum, -1.0), -1.0)
    lead_real, lead_imag = dft_pair(outer_len)
    lead_real = lead_real[:half_rows]
    lead_imag = lead_imag[:half_rows]
    scale = 1.0 / (outer_len * inner_len)
    if want_imag:
        lead = jnp.stack([jnp.stack([lead_real, lead_imag]), jnp.stack([-lead_imag, lead_real])])
    else:
        lead = jnp.stack([lead_real, lead_imag])[None]
    return jnp.einsum("qzcm,pqtz->ptcm", spectrum, lead * scale, precision=lax.Precision.HIGHEST)


def to_blocks(array):
    seq_len, chans = array.shape
    return (
        array.astype(jnp.float32).reshape(seq_len // inner_len, inner_len, chans).transpose(0, 2, 1)
    )


def from_blocks(array):
    half_rows, chans, unused = array.shape
    return array.transpose(0, 2, 1).reshape(half_rows * inner_len, chans)


def channel_work(mixed, gated, filters):
    seq_len, chans = mixed.shape
    group_count = filters.shape[0]
    group_size = chans // group_count
    half_rows = seq_len // inner_len
    outer_len = 2 * half_rows
    split_shape = (2, outer_len, group_count, group_size, inner_len)
    mix_spec = forward_spectrum(to_blocks(mixed)).reshape(split_shape)
    gate_spec = forward_spectrum(to_blocks(gated)).reshape(split_shape)
    filter_blocks = filters.reshape(group_count, half_rows, inner_len).transpose(1, 0, 2)
    filt_spec = forward_spectrum(filter_blocks)[:, :, :, None, :]
    filt_real, filt_imag = (filt_spec[0], filt_spec[1])
    mix_real, mix_imag = (mix_spec[0], mix_spec[1])
    gate_real, gate_imag = (gate_spec[0], gate_spec[1])
    conv_real = filt_real * mix_real - filt_imag * mix_imag
    conv_imag = filt_real * mix_imag + filt_imag * mix_real
    corr_real = filt_real * gate_real + filt_imag * gate_imag
    corr_imag = filt_real * gate_imag - filt_imag * gate_real
    combined = jnp.stack([conv_real - corr_imag, conv_imag + corr_real]).reshape(
        2, outer_len, chans, inner_len
    )
    both = inverse_spectrum(combined, True)
    conv_out = from_blocks(both[0])
    mixed_grad = from_blocks(both[1])
    lag_real = jnp.sum(mix_real * gate_real + mix_imag * gate_imag, axis=2)
    lag_imag = jnp.sum(mix_real * gate_imag - mix_imag * gate_real, axis=2)
    lag_out = inverse_spectrum(jnp.stack([lag_real, lag_imag]), False)[0]
    filter_grad = lag_out.transpose(1, 0, 2).reshape(group_count, seq_len) * (
        group_size * seq_len
    ) ** (-0.5)
    return (conv_out, mixed_grad, filter_grad)


def rounded_product(left, right):
    product = (left.astype(jnp.float32) * right.astype(jnp.float32)).astype(jnp.bfloat16)
    return lax.optimization_barrier(product)


def per_device(query_proj, key_proj, value_proj, cotangent, out_weight, filters):
    grad_rows = jnp.einsum(
        "tj,cj->tc",
        cotangent,
        lax.all_gather(out_weight, "ctx", axis=0, tiled=True),
        preferred_element_type=jnp.float32,
    ).astype(jnp.bfloat16)
    query_cols, key_cols, value_cols, grad_cols = (
        lax.all_to_all(query_proj, "ctx", split_axis=1, concat_axis=0, tiled=True),
        lax.all_to_all(key_proj, "ctx", split_axis=1, concat_axis=0, tiled=True),
        lax.all_to_all(value_proj, "ctx", split_axis=1, concat_axis=0, tiled=True),
        lax.all_to_all(grad_rows, "ctx", split_axis=1, concat_axis=0, tiled=True),
    )
    mixed_cols = rounded_product(key_cols, value_cols)
    gated_cols = rounded_product(query_cols, grad_cols)
    conv_out, mixed_grad, filter_grad = channel_work(mixed_cols, gated_cols, filters)
    query_grad_cols = grad_cols.astype(jnp.float32) * conv_out
    query_grad, key_grad, value_grad = (
        lax.all_to_all(query_grad_cols, "ctx", split_axis=0, concat_axis=1, tiled=True),
        lax.all_to_all(
            mixed_grad * value_cols.astype(jnp.float32),
            "ctx",
            split_axis=0,
            concat_axis=1,
            tiled=True,
        ),
        lax.all_to_all(
            mixed_grad * key_cols.astype(jnp.float32),
            "ctx",
            split_axis=0,
            concat_axis=1,
            tiled=True,
        ),
    )
    return (query_grad, key_grad, value_grad, filter_grad)


blocks = 16
lane = 128
group_size = 16


def stack_pairs(tile):
    pairs = tile.reshape(8, 2, group_size, lane)
    return jnp.concatenate(
        [pairs[:, 0].reshape(lane, lane), pairs[:, 1].reshape(lane, lane)], axis=1
    )


def shift_down(rows, count):
    if count == 0:
        return rows
    return jnp.concatenate([jnp.zeros((count, rows.shape[1]), rows.dtype), rows[:-count]], axis=0)


def shift_up(rows, count):
    if count == 0:
        return rows
    return jnp.concatenate([rows[count:], jnp.zeros((count, rows.shape[1]), rows.dtype)], axis=0)


def toeplitz(filter_row):
    seq_len = filter_row.shape[1]
    wide = jnp.broadcast_to(filter_row, (lane, seq_len))
    rolled = pltpu.roll(wide, 0, 1, stride=1, stride_axis=0)
    row_at = lax.broadcasted_iota(jnp.int32, (lane, lane), 0)
    lane_at = lax.broadcasted_iota(jnp.int32, (lane, lane), 1)
    first = jnp.where(lane_at >= row_at, rolled[:, :lane], 0.0)
    top = jnp.concatenate([first, rolled[:, lane:]], axis=1).astype(jnp.bfloat16)
    low = jnp.concatenate([jnp.zeros((lane, lane), jnp.bfloat16), top[:, :-lane]], axis=1)
    return jnp.concatenate([top, low], axis=0)


nt_dims = (((1,), (1,)), ((), ()))


def grad_block(pair, weight_ref, cot_ref, grad_ref):
    cot = cot_ref[pl.ds(2 * pair, 2)].reshape(2 * lane, cot_ref.shape[2])
    grad = lax.dot_general(weight_ref[...], cot, nt_dims, preferred_element_type=jnp.float32)
    grad = grad.astype(jnp.bfloat16)
    grad_ref[2 * pair] = grad[:, :lane]
    grad_ref[2 * pair + 1] = grad[:, lane:]


def store_pairs(out_ref, rows, value):
    value = value.reshape(8, group_size, 2 * lane)
    for index in range(8):
        out_ref[2 * index, rows, :] = value[index, :, :lane].astype(out_ref.dtype)
        out_ref[2 * index + 1, rows, :] = value[index, :, lane:].astype(out_ref.dtype)


def group_rows(group):
    return pl.ds(pl.multiple_of(group * group_size, group_size), group_size)


def conv_group(group, mixed_ref, filt_ref, toep_ref, conv_ref):
    rows = group_rows(group)
    toep = toeplitz(filt_ref[pl.ds(group, 1), :])
    toep_ref[group] = toep
    mixed = stack_pairs(mixed_ref[:, rows, :])
    left = jnp.concatenate([shift_down(mixed, group_size * step) for step in range(8)], axis=1)
    right = jnp.concatenate(
        [toep[:, 2 * lane * step : 2 * lane * (step + 1)] for step in range(8)], axis=0
    )
    store_pairs(conv_ref, rows, jnp.dot(left, right, preferred_element_type=jnp.float32))


def query_group(group, conv_ref, grad_ref, out_ref):
    rows = group_rows(group)
    out_ref[:, rows, :] = (
        conv_ref[:, rows, :] * grad_ref[:, rows, :].astype(jnp.float32)
    ).astype(out_ref.dtype)


def gated_of(rows, query_ref, grad_ref):
    return (
        query_ref[:, rows, :].astype(jnp.float32) * grad_ref[:, rows, :].astype(jnp.float32)
    ).astype(jnp.bfloat16)


def corr_group(group, query_ref, grad_ref, toep_ref, out_ref):
    rows = group_rows(group)
    gated = stack_pairs(gated_of(rows, query_ref, grad_ref))
    left = jnp.concatenate([shift_up(gated, group_size * step) for step in range(8)], axis=1)
    store_pairs(
        out_ref,
        rows,
        lax.dot_general(left, toep_ref[group], nt_dims, preferred_element_type=jnp.float32),
    )


def lag_group(group, mixed_ref, query_ref, grad_ref, lag_ref):
    rows = group_rows(group)
    gated = gated_of(rows, query_ref, grad_ref).reshape(2 * lane, lane)
    right = jnp.concatenate([shift_up(gated, group_size * step) for step in range(blocks)], axis=1)
    row_at = lax.broadcasted_iota(jnp.int32, (lane, lane), 0)
    lane_at = lax.broadcasted_iota(jnp.int32, (lane, lane), 1)
    flip = jnp.where(row_at + lane_at == lane - 1, 1.0, 0.0).astype(jnp.bfloat16)
    mixed = mixed_ref[:, rows, :].reshape(2 * lane, lane)
    left = lax.dot_general(flip, mixed, nt_dims, preferred_element_type=jnp.float32)
    cross = jnp.dot(left.astype(jnp.bfloat16), right, preferred_element_type=jnp.float32)
    cross = jnp.concatenate([cross, jnp.zeros((lane, lane), jnp.float32)], axis=1)
    rolled = pltpu.roll(cross, 0, 1, stride=1, stride_axis=0)
    lag_ref[pl.ds(group, 1), :] = jnp.sum(rolled, axis=0, keepdims=True)


def finish_lag(lag_ref, out_ref):
    seq_len = out_ref.shape[1]
    scale = (group_size * seq_len) ** -0.5
    rolled = pltpu.roll(lag_ref[...], seq_len + 1, 1)
    out_ref[...] = rolled[:, :seq_len] * scale


def channel_kernel(
    mixed_ref, query_ref, cot_ref, weight_ref, filt_ref,
    qgrad_ref, mgrad_ref, fgrad_ref,
    grad_ref, conv_ref, toep_ref, lag_ref,
):
    @pl.loop(0, 8)
    def _(pair):
        grad_block(pair, weight_ref, cot_ref, grad_ref)

    @pl.loop(0, blocks)
    def _(group):
        conv_group(group, mixed_ref, filt_ref, toep_ref, conv_ref)
        query_group(group, conv_ref, grad_ref, qgrad_ref)
        corr_group(group, query_ref, grad_ref, toep_ref, mgrad_ref)
        lag_group(group, mixed_ref, query_ref, grad_ref, lag_ref)

    finish_lag(lag_ref, fgrad_ref)


def final_kernel(qgrad_ref, mgrad_ref, key_ref, value_ref, query_out, key_out, value_out):
    query_out[...] = qgrad_ref[...].astype(jnp.float32).T
    mgrad = mgrad_ref[...].astype(jnp.float32).T
    key_out[...] = mgrad * value_ref[...].astype(jnp.float32)
    value_out[...] = mgrad * key_ref[...].astype(jnp.float32)


def finish(qgrad, mgrad, key_proj, value_proj):
    chans = key_proj.shape[1]
    wide = chans // 4
    return pl.pallas_call(
        final_kernel,
        grid=(4,),
        in_specs=[pl.BlockSpec((wide, lane), lambda i: (i, 0))] * 2
        + [pl.BlockSpec((lane, wide), lambda i: (0, i))] * 2,
        out_specs=[pl.BlockSpec((lane, wide), lambda i: (0, i))] * 3,
        out_shape=[jax.ShapeDtypeStruct(key_proj.shape, jnp.float32)] * 3,
        compiler_params=pltpu.CompilerParams(vmem_limit_bytes=32 * 1024 * 1024),
        cost_estimate=pl.CostEstimate(flops=1 << 20, bytes_accessed=10 << 20, transcendentals=0),
    )(qgrad.reshape(chans, lane), mgrad.reshape(chans, lane), key_proj, value_proj)


def direct_device(query_proj, key_proj, value_proj, cotangent, out_weight, filters):
    own = out_weight.shape[0]
    features = cotangent.shape[1]
    seq_len = filters.shape[1]
    tile_shape = (blocks, own, lane)
    mixed = rounded_product(key_proj, value_proj).T.reshape(tile_shape)
    query = query_proj.T.reshape(tile_shape)
    mixed_cols = lax.all_to_all(mixed, "ctx", split_axis=0, concat_axis=0, tiled=True)
    query_cols = lax.all_to_all(query, "ctx", split_axis=0, concat_axis=0, tiled=True)
    cot_all = lax.all_gather(cotangent, "ctx", axis=0, tiled=True).reshape(blocks, lane, features)
    vmem = pl.BlockSpec(memory_space=pltpu.VMEM)
    qgrad, mgrad, filter_grad = pl.pallas_call(
        channel_kernel,
        in_specs=[vmem] * 5,
        out_specs=[vmem] * 3,
        out_shape=[
            jax.ShapeDtypeStruct(tile_shape, jnp.bfloat16),
            jax.ShapeDtypeStruct(tile_shape, jnp.bfloat16),
            jax.ShapeDtypeStruct(filters.shape, jnp.float32),
        ],
        scratch_shapes=[
            pltpu.VMEM(tile_shape, jnp.bfloat16),
            pltpu.VMEM(tile_shape, jnp.float32),
            pltpu.VMEM((blocks, 2 * lane, seq_len), jnp.bfloat16),
            pltpu.VMEM((filters.shape[0], seq_len + lane), jnp.float32),
        ],
        compiler_params=pltpu.CompilerParams(vmem_limit_bytes=52 * 1024 * 1024),
        cost_estimate=pl.CostEstimate(
            flops=8 << 30, bytes_accessed=16 << 20, transcendentals=0
        ),
    )(mixed_cols, query_cols, cot_all, out_weight, filters)
    qgrad = lax.all_to_all(qgrad, "ctx", split_axis=0, concat_axis=0, tiled=True)
    mgrad = lax.all_to_all(mgrad, "ctx", split_axis=0, concat_axis=0, tiled=True)
    return (*finish(qgrad, mgrad, key_proj, value_proj), filter_grad)


def solution(mesh):
    placed = (
        P(("parts", "ctx"), None),
        P(("parts", "ctx"), None),
        P(("parts", "ctx"), None),
        P(("parts", "ctx"), None),
        P("ctx", None),
        P("ctx", None),
    )
    work = direct_device if mesh.shape["ctx"] == blocks else per_device
    return jax.shard_map(
        work,
        mesh=mesh,
        in_specs=placed,
        out_specs=(
            P(("parts", "ctx"), None),
            P(("parts", "ctx"), None),
            P(("parts", "ctx"), None),
            P(("parts", "ctx"), None),
        ),
        check_vma=False,
    )
```

```python
import math

import jax
import jax.numpy as jnp
from jax import lax
from jax.experimental import pallas as pl
from jax.experimental.pallas import tpu as pltpu
from jax.sharding import PartitionSpec as P

inner_len = 128


def dft_pair(size_count):
    index_row = jnp.arange(size_count, dtype=jnp.int32)
    phase = (index_row[:, None] * index_row[None, :] % size_count).astype(jnp.float32) * (
        -2.0 * math.pi / size_count
    )
    return (jnp.cos(phase), jnp.sin(phase))


def twist(spectrum, sign):
    outer_len = spectrum.shape[1]
    total = outer_len * inner_len
    outer_index = jnp.arange(outer_len, dtype=jnp.int32)[:, None, None]
    inner_index = jnp.arange(inner_len, dtype=jnp.int32)[None, None, :]
    phase = (outer_index * inner_index % total).astype(jnp.float32) * (-2.0 * math.pi / total)
    tw_real = jnp.cos(phase)
    tw_imag = jnp.sin(phase) * sign
    real_part = spectrum[0] * tw_real - spectrum[1] * tw_imag
    imag_part = spectrum[0] * tw_imag + spectrum[1] * tw_real
    return jnp.stack([real_part, imag_part])


def last_matrix(sign):
    last_real, last_imag = dft_pair(inner_len)
    last_imag = last_imag * sign
    return jnp.stack([jnp.stack([last_real, -last_imag]), jnp.stack([last_imag, last_real])])


def apply_last(spectrum, sign):
    return jnp.einsum(
        "qzcn,pqkn->pzck", spectrum, last_matrix(sign), precision=lax.Precision.HIGHEST
    )


def forward_spectrum(signal):
    half_rows = signal.shape[0]
    outer_len = 2 * half_rows
    lead_real, lead_imag = dft_pair(outer_len)
    lead = jnp.stack([lead_real[:, :half_rows], lead_imag[:, :half_rows]])
    spectrum = jnp.einsum("pzn,ncm->pzcm", lead, signal, precision=lax.Precision.HIGHEST)
    return apply_last(twist(spectrum, 1.0), 1.0)


def inverse_spectrum(spectrum, want_imag):
    outer_len = spectrum.shape[1]
    half_rows = outer_len // 2
    spectrum = twist(apply_last(spectrum, -1.0), -1.0)
    lead_real, lead_imag = dft_pair(outer_len)
    lead_real = lead_real[:half_rows]
    lead_imag = lead_imag[:half_rows]
    scale = 1.0 / (outer_len * inner_len)
    if want_imag:
        lead = jnp.stack([jnp.stack([lead_real, lead_imag]), jnp.stack([-lead_imag, lead_real])])
    else:
        lead = jnp.stack([lead_real, lead_imag])[None]
    return jnp.einsum("qzcm,pqtz->ptcm", spectrum, lead * scale, precision=lax.Precision.HIGHEST)


def to_blocks(array):
    seq_len, chans = array.shape
    return (
        array.astype(jnp.float32).reshape(seq_len // inner_len, inner_len, chans).transpose(0, 2, 1)
    )


def from_blocks(array):
    half_rows, chans, unused = array.shape
    return array.transpose(0, 2, 1).reshape(half_rows * inner_len, chans)


def channel_work(mixed, gated, filters):
    seq_len, chans = mixed.shape
    group_count = filters.shape[0]
    group_size = chans // group_count
    half_rows = seq_len // inner_len
    outer_len = 2 * half_rows
    split_shape = (2, outer_len, group_count, group_size, inner_len)
    mix_spec = forward_spectrum(to_blocks(mixed)).reshape(split_shape)
    gate_spec = forward_spectrum(to_blocks(gated)).reshape(split_shape)
    filter_blocks = filters.reshape(group_count, half_rows, inner_len).transpose(1, 0, 2)
    filt_spec = forward_spectrum(filter_blocks)[:, :, :, None, :]
    filt_real, filt_imag = (filt_spec[0], filt_spec[1])
    mix_real, mix_imag = (mix_spec[0], mix_spec[1])
    gate_real, gate_imag = (gate_spec[0], gate_spec[1])
    conv_real = filt_real * mix_real - filt_imag * mix_imag
    conv_imag = filt_real * mix_imag + filt_imag * mix_real
    corr_real = filt_real * gate_real + filt_imag * gate_imag
    corr_imag = filt_real * gate_imag - filt_imag * gate_real
    combined = jnp.stack([conv_real - corr_imag, conv_imag + corr_real]).reshape(
        2, outer_len, chans, inner_len
    )
    both = inverse_spectrum(combined, True)
    conv_out = from_blocks(both[0])
    mixed_grad = from_blocks(both[1])
    lag_real = jnp.sum(mix_real * gate_real + mix_imag * gate_imag, axis=2)
    lag_imag = jnp.sum(mix_real * gate_imag - mix_imag * gate_real, axis=2)
    lag_out = inverse_spectrum(jnp.stack([lag_real, lag_imag]), False)[0]
    filter_grad = lag_out.transpose(1, 0, 2).reshape(group_count, seq_len) * (
        group_size * seq_len
    ) ** (-0.5)
    return (conv_out, mixed_grad, filter_grad)


def rounded_product(left, right):
    product = (left.astype(jnp.float32) * right.astype(jnp.float32)).astype(jnp.bfloat16)
    return lax.optimization_barrier(product)


def per_device(query_proj, key_proj, value_proj, cotangent, out_weight, filters):
    grad_rows = jnp.einsum(
        "tj,cj->tc",
        cotangent,
        lax.all_gather(out_weight, "ctx", axis=0, tiled=True),
        preferred_element_type=jnp.float32,
    ).astype(jnp.bfloat16)
    query_cols, key_cols, value_cols, grad_cols = (
        lax.all_to_all(query_proj, "ctx", split_axis=1, concat_axis=0, tiled=True),
        lax.all_to_all(key_proj, "ctx", split_axis=1, concat_axis=0, tiled=True),
        lax.all_to_all(value_proj, "ctx", split_axis=1, concat_axis=0, tiled=True),
        lax.all_to_all(grad_rows, "ctx", split_axis=1, concat_axis=0, tiled=True),
    )
    mixed_cols = rounded_product(key_cols, value_cols)
    gated_cols = rounded_product(query_cols, grad_cols)
    conv_out, mixed_grad, filter_grad = channel_work(mixed_cols, gated_cols, filters)
    query_grad_cols = grad_cols.astype(jnp.float32) * conv_out
    query_grad, key_grad, value_grad = (
        lax.all_to_all(query_grad_cols, "ctx", split_axis=0, concat_axis=1, tiled=True),
        lax.all_to_all(
            mixed_grad * value_cols.astype(jnp.float32),
            "ctx",
            split_axis=0,
            concat_axis=1,
            tiled=True,
        ),
        lax.all_to_all(
            mixed_grad * key_cols.astype(jnp.float32),
            "ctx",
            split_axis=0,
            concat_axis=1,
            tiled=True,
        ),
    )
    return (query_grad, key_grad, value_grad, filter_grad)


blocks = 16
lane = 128
group_size = 16


def stack_pairs(tile):
    pairs = tile.reshape(8, 2, group_size, lane)
    return jnp.concatenate(
        [pairs[:, 0].reshape(lane, lane), pairs[:, 1].reshape(lane, lane)], axis=1
    )


def shift_down(rows, count):
    if count == 0:
        return rows
    return jnp.concatenate([jnp.zeros((count, rows.shape[1]), rows.dtype), rows[:-count]], axis=0)


def shift_up(rows, count):
    if count == 0:
        return rows
    return jnp.concatenate([rows[count:], jnp.zeros((count, rows.shape[1]), rows.dtype)], axis=0)


def toeplitz(filter_row):
    seq_len = filter_row.shape[1]
    wide = jnp.broadcast_to(filter_row, (lane, seq_len))
    rolled = pltpu.roll(wide, 0, 1, stride=1, stride_axis=0)
    row_at = lax.broadcasted_iota(jnp.int32, (lane, lane), 0)
    lane_at = lax.broadcasted_iota(jnp.int32, (lane, lane), 1)
    first = jnp.where(lane_at >= row_at, rolled[:, :lane], 0.0)
    top = jnp.concatenate([first, rolled[:, lane:]], axis=1).astype(jnp.bfloat16)
    low = jnp.concatenate([jnp.zeros((lane, lane), jnp.bfloat16), top[:, :-lane]], axis=1)
    return jnp.concatenate([top, low], axis=0)


nt_dims = (((1,), (1,)), ((), ()))


def grad_block(pair, weight_ref, cot_ref, grad_ref):
    cot = cot_ref[pl.ds(2 * pair, 2)].reshape(2 * lane, cot_ref.shape[2])
    grad = lax.dot_general(weight_ref[...], cot, nt_dims, preferred_element_type=jnp.float32)
    grad = grad.astype(jnp.bfloat16)
    grad_ref[2 * pair] = grad[:, :lane]
    grad_ref[2 * pair + 1] = grad[:, lane:]


def store_pairs(out_ref, rows, value):
    value = value.reshape(8, group_size, 2 * lane)
    for index in range(8):
        out_ref[2 * index, rows, :] = value[index, :, :lane].astype(out_ref.dtype)
        out_ref[2 * index + 1, rows, :] = value[index, :, lane:].astype(out_ref.dtype)


def group_rows(group):
    return pl.ds(pl.multiple_of(group * group_size, group_size), group_size)


def conv_group(group, mixed_ref, toep_ref, conv_ref):
    rows = group_rows(group)
    toep = toep_ref[group]
    mixed = stack_pairs(mixed_ref[:, rows, :])
    left = jnp.concatenate([shift_down(mixed, group_size * step) for step in range(8)], axis=1)
    right = jnp.concatenate(
        [toep[:, 2 * lane * step : 2 * lane * (step + 1)] for step in range(8)], axis=0
    )
    store_pairs(conv_ref, rows, jnp.dot(left, right, preferred_element_type=jnp.float32))


def query_group(group, conv_ref, grad_ref, out_ref):
    rows = group_rows(group)
    out_ref[:, rows, :] = (
        conv_ref[:, rows, :] * grad_ref[:, rows, :].astype(jnp.float32)
    ).astype(out_ref.dtype)


def gated_of(rows, query_ref, grad_ref):
    return (
        query_ref[:, rows, :].astype(jnp.float32) * grad_ref[:, rows, :].astype(jnp.float32)
    ).astype(jnp.bfloat16)


def corr_group(group, query_ref, grad_ref, toep_ref, out_ref):
    rows = group_rows(group)
    gated = stack_pairs(gated_of(rows, query_ref, grad_ref))
    left = jnp.concatenate([shift_up(gated, group_size * step) for step in range(8)], axis=1)
    store_pairs(
        out_ref,
        rows,
        lax.dot_general(left, toep_ref[group], nt_dims, preferred_element_type=jnp.float32),
    )


def lag_group(group, mixed_ref, query_ref, grad_ref, lag_ref):
    rows = group_rows(group)
    gated = gated_of(rows, query_ref, grad_ref).reshape(2 * lane, lane)
    right = jnp.concatenate([shift_up(gated, group_size * step) for step in range(blocks)], axis=1)
    row_at = lax.broadcasted_iota(jnp.int32, (lane, lane), 0)
    lane_at = lax.broadcasted_iota(jnp.int32, (lane, lane), 1)
    flip = jnp.where(row_at + lane_at == lane - 1, 1.0, 0.0).astype(jnp.bfloat16)
    mixed = mixed_ref[:, rows, :].reshape(2 * lane, lane)
    left = lax.dot_general(flip, mixed, nt_dims, preferred_element_type=jnp.float32)
    cross = jnp.dot(left.astype(jnp.bfloat16), right, preferred_element_type=jnp.float32)
    cross = jnp.concatenate([cross, jnp.zeros((lane, lane), jnp.float32)], axis=1)
    rolled = pltpu.roll(cross, 0, 1, stride=1, stride_axis=0)
    lag_ref[pl.ds(group, 1), :] = jnp.sum(rolled, axis=0, keepdims=True)


def finish_lag(lag_ref, out_ref):
    seq_len = out_ref.shape[1]
    scale = (group_size * seq_len) ** -0.5
    rolled = pltpu.roll(lag_ref[...], seq_len + 1, 1)
    out_ref[...] = rolled[:, :seq_len] * scale


def remote(src, dst, send, recv, peer):
    return pltpu.make_async_remote_copy(
        src_ref=src,
        dst_ref=dst,
        send_sem=send,
        recv_sem=recv,
        device_id={"ctx": peer},
        device_id_type=pl.DeviceIdType.MESH,
    )


def slice_kernel(
    mixed_ref, query_ref, cot_ref, weight_ref, filt_ref,
    qback_ref, mback_ref, fgrad_ref,
    mixed_in, query_in, cot_in, qgrad_ref, mgrad_ref, grad_ref, conv_ref, toep_ref, lag_ref,
    cot_send, cot_recv, mixed_send, mixed_recv, query_send, query_recv,
    qback_send, qback_recv, mback_send, mback_recv, local_sem,
):
    me = lax.axis_index("ctx")
    place_z, place_y, place_core = me // 4, (me // 2) % 2, me % 2
    y_peer = me + 2 - 4 * place_y
    core_peer = me + 1 - 2 * place_core

    def peer_of(step):
        return (me + step) % blocks

    barrier = pltpu.get_barrier_semaphore()

    @pl.loop(1, blocks)
    def _(step):
        pl.semaphore_signal(
            barrier, inc=1, device_id={"ctx": peer_of(step)}, device_id_type=pl.DeviceIdType.MESH
        )

    pl.semaphore_wait(barrier, blocks - 1)

    def cot_copy(src, block, way, peer):
        return remote(src, cot_in.at[block], cot_send.at[way, block], cot_recv.at[block], peer)

    def forward(src, block, ways, act):
        if "u" in ways:
            @pl.when(place_z < 3)
            def _():
                act(cot_copy(src, block, 0, me + 4))
        if "d" in ways:
            @pl.when(place_z > 0)
            def _():
                act(cot_copy(src, block, 1, me - 4))
        if "y" in ways:
            act(cot_copy(src, block, 2, y_peer))
        if "c" in ways:
            act(cot_copy(src, block, 3, core_peer))

    def arrived(block):
        cot_copy(cot_in.at[block], block, 3, core_peer).wait_recv()

    def begin(copy):
        copy.start()

    def sent(copy):
        copy.wait_send()

    def relay_z(hop, act, wait):
        @pl.when(place_z >= hop)
        def _():
            block = me - 4 * hop
            if wait:
                arrived(block)
            forward(cot_in.at[block], block, "uyc", act)

        @pl.when(place_z + hop <= 3)
        def _():
            block = me + 4 * hop
            if wait:
                arrived(block)
            forward(cot_in.at[block], block, "dyc", act)

    def relay_y(hop, act, wait):
        def one(block):
            if wait:
                arrived(block)
            forward(cot_in.at[block], block, "c", act)

        if hop == 0:
            one(y_peer)
        else:
            @pl.when(place_z >= hop)
            def _():
                one(y_peer - 4 * hop)

            @pl.when(place_z + hop <= 3)
            def _():
                one(y_peer + 4 * hop)

    def start_all(src, dst, send, recv, local, rows):
        pltpu.make_async_copy(src.at[me, rows], dst.at[me, rows], local).start()

        @pl.loop(1, blocks)
        def _(step):
            peer = peer_of(step)
            remote(src.at[peer, rows], dst.at[me, rows], send.at[peer], recv.at[me], peer).start()

    def wait_arrivals(src, dst, send, recv, local, rows):
        pltpu.make_async_copy(src.at[me, rows], dst.at[me, rows], local).wait()

        @pl.loop(1, blocks)
        def _(step):
            peer = peer_of(step)
            remote(
                src.at[peer, rows], dst.at[peer, rows], send.at[peer], recv.at[peer], peer
            ).wait_recv()

    def wait_sends(src, dst, send, recv, local, rows):
        @pl.loop(1, blocks)
        def _(step):
            peer = peer_of(step)
            remote(
                src.at[peer, rows], dst.at[me, rows], send.at[peer], recv.at[me], peer
            ).wait_send()

    every = pl.ds(0, mixed_in.shape[1])
    mixed_trip = (mixed_ref, mixed_in, mixed_send, mixed_recv, local_sem.at[0], every)
    query_trip = (query_ref, query_in, query_send, query_recv, local_sem.at[1], every)
    qback_trip = (qgrad_ref, qback_ref, qback_send, qback_recv, local_sem.at[2], every)
    halves = 2
    half_rows = mixed_in.shape[1] // halves
    mback_trips = [
        (
            mgrad_ref, mback_ref, mback_send.at[half], mback_recv.at[half],
            local_sem.at[4 + half], pl.ds(half * half_rows, half_rows),
        )
        for half in range(halves)
    ]

    forward(cot_ref, me, "udyc", begin)
    own_cot = pltpu.make_async_copy(cot_ref, cot_in.at[me], local_sem.at[3])
    own_cot.start()
    start_all(*mixed_trip)

    @pl.loop(0, blocks)
    def _(group):
        toep_ref[group] = toeplitz(filt_ref[pl.ds(group, 1), :])

    relay_z(1, begin, True)
    relay_y(0, begin, True)
    relay_z(2, begin, True)
    relay_y(1, begin, True)
    start_all(*query_trip)
    relay_z(3, begin, True)
    wait_arrivals(*mixed_trip)

    @pl.loop(0, blocks)
    def _(group):
        conv_group(group, mixed_in, toep_ref, conv_ref)

    relay_y(2, begin, True)
    relay_y(3, begin, True)
    own_cot.wait()

    @pl.loop(0, blocks // 2)
    def _(pair):
        arrived(2 * pair + 1 - place_core)

    @pl.loop(0, blocks // 2)
    def _(pair):
        grad_block(pair, weight_ref, cot_in, grad_ref)

    @pl.loop(0, blocks)
    def _(group):
        query_group(group, conv_ref, grad_ref, qgrad_ref)

    start_all(*qback_trip)
    wait_arrivals(*query_trip)
    for half in range(halves):
        @pl.loop(half * blocks // halves, (half + 1) * blocks // halves)
        def _(group):
            corr_group(group, query_in, grad_ref, toep_ref, mgrad_ref)

        start_all(*mback_trips[half])

    @pl.loop(0, blocks)
    def _(group):
        lag_group(group, mixed_in, query_in, grad_ref, lag_ref)

    finish_lag(lag_ref, fgrad_ref)

    forward(cot_ref, me, "udyc", sent)
    for hop in (1, 2, 3):
        relay_z(hop, sent, False)
    for hop in (0, 1, 2, 3):
        relay_y(hop, sent, False)
    for trip in [mixed_trip, query_trip, qback_trip] + mback_trips:
        wait_sends(*trip)
    for trip in [qback_trip] + mback_trips:
        wait_arrivals(*trip)


def final_kernel(qgrad_ref, mgrad_ref, key_ref, value_ref, query_out, key_out, value_out):
    query_out[...] = qgrad_ref[...].astype(jnp.float32).T
    mgrad = mgrad_ref[...].astype(jnp.float32).T
    key_out[...] = mgrad * value_ref[...].astype(jnp.float32)
    value_out[...] = mgrad * key_ref[...].astype(jnp.float32)


def finish(qgrad, mgrad, key_proj, value_proj):
    chans = key_proj.shape[1]
    wide = chans // 4
    return pl.pallas_call(
        final_kernel,
        grid=(4,),
        in_specs=[pl.BlockSpec((wide, lane), lambda i: (i, 0))] * 2
        + [pl.BlockSpec((lane, wide), lambda i: (0, i))] * 2,
        out_specs=[pl.BlockSpec((lane, wide), lambda i: (0, i))] * 3,
        out_shape=[jax.ShapeDtypeStruct(key_proj.shape, jnp.float32)] * 3,
        compiler_params=pltpu.CompilerParams(vmem_limit_bytes=32 * 1024 * 1024),
        cost_estimate=pl.CostEstimate(flops=1 << 20, bytes_accessed=10 << 20, transcendentals=0),
    )(qgrad.reshape(chans, lane), mgrad.reshape(chans, lane), key_proj, value_proj)


def direct_device(query_proj, key_proj, value_proj, cotangent, out_weight, filters):
    own = out_weight.shape[0]
    features = cotangent.shape[1]
    seq_len = filters.shape[1]
    tile_shape = (blocks, own, lane)
    mixed = rounded_product(key_proj, value_proj).T.reshape(tile_shape)
    query = query_proj.T.reshape(tile_shape)
    vmem = pl.BlockSpec(memory_space=pltpu.VMEM)
    anywhere = pl.BlockSpec(memory_space=pl.ANY)
    dma = pltpu.SemaphoreType.DMA
    tile = pltpu.VMEM(tile_shape, jnp.bfloat16)
    qgrad, mgrad, filter_grad = pl.pallas_call(
        slice_kernel,
        in_specs=[anywhere] * 3 + [vmem] * 2,
        out_specs=[anywhere] * 2 + [vmem],
        out_shape=[
            jax.ShapeDtypeStruct(tile_shape, jnp.bfloat16),
            jax.ShapeDtypeStruct(tile_shape, jnp.bfloat16),
            jax.ShapeDtypeStruct(filters.shape, jnp.float32),
        ],
        scratch_shapes=[
            tile,
            tile,
            pltpu.VMEM((blocks, lane, features), jnp.bfloat16),
            tile,
            tile,
            tile,
            pltpu.VMEM(tile_shape, jnp.float32),
            pltpu.VMEM((blocks, 2 * lane, seq_len), jnp.bfloat16),
            pltpu.VMEM((filters.shape[0], seq_len + lane), jnp.float32),
            dma((4, blocks)),
            dma((blocks,)),
            dma((blocks,)),
            dma((blocks,)),
            dma((blocks,)),
            dma((blocks,)),
            dma((blocks,)),
            dma((blocks,)),
            dma((2, blocks)),
            dma((2, blocks)),
            dma((6,)),
        ],
        compiler_params=pltpu.CompilerParams(
            collective_id=0, has_side_effects=True, vmem_limit_bytes=52 * 1024 * 1024
        ),
        cost_estimate=pl.CostEstimate(
            flops=8 << 30, bytes_accessed=16 << 20, transcendentals=0
        ),
    )(mixed, query, cotangent, out_weight, filters)
    return (*finish(qgrad, mgrad, key_proj, value_proj), filter_grad)


def solution(mesh):
    placed = (
        P(("parts", "ctx"), None),
        P(("parts", "ctx"), None),
        P(("parts", "ctx"), None),
        P(("parts", "ctx"), None),
        P("ctx", None),
        P("ctx", None),
    )
    work = direct_device if mesh.shape["ctx"] == blocks else per_device
    return jax.shard_map(
        work,
        mesh=mesh,
        in_specs=placed,
        out_specs=(
            P(("parts", "ctx"), None),
            P(("parts", "ctx"), None),
            P(("parts", "ctx"), None),
            P(("parts", "ctx"), None),
        ),
        check_vma=False,
    )
```

```python
import math

import jax
import jax.numpy as jnp
from jax import lax
from jax.experimental import pallas as pl
from jax.experimental.pallas import tpu as pltpu
from jax.sharding import PartitionSpec as P

inner_len = 128


def dft_pair(size_count):
    index_row = jnp.arange(size_count, dtype=jnp.int32)
    phase = (index_row[:, None] * index_row[None, :] % size_count).astype(jnp.float32) * (
        -2.0 * math.pi / size_count
    )
    return (jnp.cos(phase), jnp.sin(phase))


def twist(spectrum, sign):
    outer_len = spectrum.shape[1]
    total = outer_len * inner_len
    outer_index = jnp.arange(outer_len, dtype=jnp.int32)[:, None, None]
    inner_index = jnp.arange(inner_len, dtype=jnp.int32)[None, None, :]
    phase = (outer_index * inner_index % total).astype(jnp.float32) * (-2.0 * math.pi / total)
    tw_real = jnp.cos(phase)
    tw_imag = jnp.sin(phase) * sign
    real_part = spectrum[0] * tw_real - spectrum[1] * tw_imag
    imag_part = spectrum[0] * tw_imag + spectrum[1] * tw_real
    return jnp.stack([real_part, imag_part])


def last_matrix(sign):
    last_real, last_imag = dft_pair(inner_len)
    last_imag = last_imag * sign
    return jnp.stack([jnp.stack([last_real, -last_imag]), jnp.stack([last_imag, last_real])])


def apply_last(spectrum, sign):
    return jnp.einsum(
        "qzcn,pqkn->pzck", spectrum, last_matrix(sign), precision=lax.Precision.HIGHEST
    )


def forward_spectrum(signal):
    half_rows = signal.shape[0]
    outer_len = 2 * half_rows
    lead_real, lead_imag = dft_pair(outer_len)
    lead = jnp.stack([lead_real[:, :half_rows], lead_imag[:, :half_rows]])
    spectrum = jnp.einsum("pzn,ncm->pzcm", lead, signal, precision=lax.Precision.HIGHEST)
    return apply_last(twist(spectrum, 1.0), 1.0)


def inverse_spectrum(spectrum, want_imag):
    outer_len = spectrum.shape[1]
    half_rows = outer_len // 2
    spectrum = twist(apply_last(spectrum, -1.0), -1.0)
    lead_real, lead_imag = dft_pair(outer_len)
    lead_real = lead_real[:half_rows]
    lead_imag = lead_imag[:half_rows]
    scale = 1.0 / (outer_len * inner_len)
    if want_imag:
        lead = jnp.stack([jnp.stack([lead_real, lead_imag]), jnp.stack([-lead_imag, lead_real])])
    else:
        lead = jnp.stack([lead_real, lead_imag])[None]
    return jnp.einsum("qzcm,pqtz->ptcm", spectrum, lead * scale, precision=lax.Precision.HIGHEST)


def to_blocks(array):
    seq_len, chans = array.shape
    return (
        array.astype(jnp.float32).reshape(seq_len // inner_len, inner_len, chans).transpose(0, 2, 1)
    )


def from_blocks(array):
    half_rows, chans, unused = array.shape
    return array.transpose(0, 2, 1).reshape(half_rows * inner_len, chans)


def channel_work(mixed, gated, filters):
    seq_len, chans = mixed.shape
    group_count = filters.shape[0]
    group_size = chans // group_count
    half_rows = seq_len // inner_len
    outer_len = 2 * half_rows
    split_shape = (2, outer_len, group_count, group_size, inner_len)
    mix_spec = forward_spectrum(to_blocks(mixed)).reshape(split_shape)
    gate_spec = forward_spectrum(to_blocks(gated)).reshape(split_shape)
    filter_blocks = filters.reshape(group_count, half_rows, inner_len).transpose(1, 0, 2)
    filt_spec = forward_spectrum(filter_blocks)[:, :, :, None, :]
    filt_real, filt_imag = (filt_spec[0], filt_spec[1])
    mix_real, mix_imag = (mix_spec[0], mix_spec[1])
    gate_real, gate_imag = (gate_spec[0], gate_spec[1])
    conv_real = filt_real * mix_real - filt_imag * mix_imag
    conv_imag = filt_real * mix_imag + filt_imag * mix_real
    corr_real = filt_real * gate_real + filt_imag * gate_imag
    corr_imag = filt_real * gate_imag - filt_imag * gate_real
    combined = jnp.stack([conv_real - corr_imag, conv_imag + corr_real]).reshape(
        2, outer_len, chans, inner_len
    )
    both = inverse_spectrum(combined, True)
    conv_out = from_blocks(both[0])
    mixed_grad = from_blocks(both[1])
    lag_real = jnp.sum(mix_real * gate_real + mix_imag * gate_imag, axis=2)
    lag_imag = jnp.sum(mix_real * gate_imag - mix_imag * gate_real, axis=2)
    lag_out = inverse_spectrum(jnp.stack([lag_real, lag_imag]), False)[0]
    filter_grad = lag_out.transpose(1, 0, 2).reshape(group_count, seq_len) * (
        group_size * seq_len
    ) ** (-0.5)
    return (conv_out, mixed_grad, filter_grad)


def rounded_product(left, right):
    product = (left.astype(jnp.float32) * right.astype(jnp.float32)).astype(jnp.bfloat16)
    return lax.optimization_barrier(product)


def per_device(query_proj, key_proj, value_proj, cotangent, out_weight, filters):
    grad_rows = jnp.einsum(
        "tj,cj->tc",
        cotangent,
        lax.all_gather(out_weight, "ctx", axis=0, tiled=True),
        preferred_element_type=jnp.float32,
    ).astype(jnp.bfloat16)
    query_cols, key_cols, value_cols, grad_cols = (
        lax.all_to_all(query_proj, "ctx", split_axis=1, concat_axis=0, tiled=True),
        lax.all_to_all(key_proj, "ctx", split_axis=1, concat_axis=0, tiled=True),
        lax.all_to_all(value_proj, "ctx", split_axis=1, concat_axis=0, tiled=True),
        lax.all_to_all(grad_rows, "ctx", split_axis=1, concat_axis=0, tiled=True),
    )
    mixed_cols = rounded_product(key_cols, value_cols)
    gated_cols = rounded_product(query_cols, grad_cols)
    conv_out, mixed_grad, filter_grad = channel_work(mixed_cols, gated_cols, filters)
    query_grad_cols = grad_cols.astype(jnp.float32) * conv_out
    query_grad, key_grad, value_grad = (
        lax.all_to_all(query_grad_cols, "ctx", split_axis=0, concat_axis=1, tiled=True),
        lax.all_to_all(
            mixed_grad * value_cols.astype(jnp.float32),
            "ctx",
            split_axis=0,
            concat_axis=1,
            tiled=True,
        ),
        lax.all_to_all(
            mixed_grad * key_cols.astype(jnp.float32),
            "ctx",
            split_axis=0,
            concat_axis=1,
            tiled=True,
        ),
    )
    return (query_grad, key_grad, value_grad, filter_grad)


blocks = 16
lane = 128
group_size = 16


def stack_pairs(tile):
    pairs = tile.reshape(8, 2, group_size, lane)
    return jnp.concatenate(
        [pairs[:, 0].reshape(lane, lane), pairs[:, 1].reshape(lane, lane)], axis=1
    )


def shift_down(rows, count):
    if count == 0:
        return rows
    return jnp.concatenate([jnp.zeros((count, rows.shape[1]), rows.dtype), rows[:-count]], axis=0)


def shift_up(rows, count):
    if count == 0:
        return rows
    return jnp.concatenate([rows[count:], jnp.zeros((count, rows.shape[1]), rows.dtype)], axis=0)


def toeplitz(filter_row):
    seq_len = filter_row.shape[1]
    wide = jnp.broadcast_to(filter_row, (lane, seq_len))
    rolled = pltpu.roll(wide, 0, 1, stride=1, stride_axis=0)
    row_at = lax.broadcasted_iota(jnp.int32, (lane, lane), 0)
    lane_at = lax.broadcasted_iota(jnp.int32, (lane, lane), 1)
    first = jnp.where(lane_at >= row_at, rolled[:, :lane], 0.0)
    top = jnp.concatenate([first, rolled[:, lane:]], axis=1).astype(jnp.bfloat16)
    low = jnp.concatenate([jnp.zeros((lane, lane), jnp.bfloat16), top[:, :-lane]], axis=1)
    return jnp.concatenate([top, low], axis=0)


nt_dims = (((1,), (1,)), ((), ()))


def grad_block(pair, weight_ref, cot_ref, grad_ref):
    cot = cot_ref[pl.ds(2 * pair, 2)].reshape(2 * lane, cot_ref.shape[2])
    grad = lax.dot_general(weight_ref[...], cot, nt_dims, preferred_element_type=jnp.float32)
    grad = grad.astype(jnp.bfloat16)
    grad_ref[2 * pair] = grad[:, :lane]
    grad_ref[2 * pair + 1] = grad[:, lane:]


def store_pairs(out_ref, rows, value):
    value = value.reshape(8, group_size, 2 * lane)
    for index in range(8):
        out_ref[2 * index, rows, :] = value[index, :, :lane].astype(out_ref.dtype)
        out_ref[2 * index + 1, rows, :] = value[index, :, lane:].astype(out_ref.dtype)


def group_rows(group):
    return pl.ds(pl.multiple_of(group * group_size, group_size), group_size)


def conv_group(group, mixed_ref, toep_ref, conv_ref):
    rows = group_rows(group)
    toep = toep_ref[group]
    mixed = stack_pairs(mixed_ref[:, rows, :])
    left = jnp.concatenate([shift_down(mixed, group_size * step) for step in range(8)], axis=1)
    right = jnp.concatenate(
        [toep[:, 2 * lane * step : 2 * lane * (step + 1)] for step in range(8)], axis=0
    )
    store_pairs(conv_ref, rows, jnp.dot(left, right, preferred_element_type=jnp.float32))


def gated_of(rows, query_ref, grad_ref):
    return (
        query_ref[:, rows, :].astype(jnp.float32) * grad_ref[:, rows, :].astype(jnp.float32)
    ).astype(jnp.bfloat16)


def corr_group(group, query_ref, grad_ref, toep_ref, out_ref):
    rows = group_rows(group)
    gated = stack_pairs(gated_of(rows, query_ref, grad_ref))
    left = jnp.concatenate([shift_up(gated, group_size * step) for step in range(8)], axis=1)
    store_pairs(
        out_ref,
        rows,
        lax.dot_general(left, toep_ref[group], nt_dims, preferred_element_type=jnp.float32),
    )


def lag_group(group, mixed_ref, query_ref, grad_ref, lag_ref):
    rows = group_rows(group)
    gated = gated_of(rows, query_ref, grad_ref).reshape(2 * lane, lane)
    right = jnp.concatenate([shift_up(gated, group_size * step) for step in range(blocks)], axis=1)
    row_at = lax.broadcasted_iota(jnp.int32, (lane, lane), 0)
    lane_at = lax.broadcasted_iota(jnp.int32, (lane, lane), 1)
    flip = jnp.where(row_at + lane_at == lane - 1, 1.0, 0.0).astype(jnp.bfloat16)
    mixed = mixed_ref[:, rows, :].reshape(2 * lane, lane)
    left = lax.dot_general(flip, mixed, nt_dims, preferred_element_type=jnp.float32)
    cross = jnp.dot(left.astype(jnp.bfloat16), right, preferred_element_type=jnp.float32)
    cross = jnp.concatenate([cross, jnp.zeros((lane, lane), jnp.float32)], axis=1)
    rolled = pltpu.roll(cross, 0, 1, stride=1, stride_axis=0)
    lag_ref[pl.ds(group, 1), :] = jnp.sum(rolled, axis=0, keepdims=True)


def finish_lag(lag_ref, out_ref):
    seq_len = out_ref.shape[1]
    scale = (group_size * seq_len) ** -0.5
    rolled = pltpu.roll(lag_ref[...], seq_len + 1, 1)
    out_ref[...] = rolled[:, :seq_len] * scale


def remote(src, dst, send, recv, peer):
    return pltpu.make_async_remote_copy(
        src_ref=src,
        dst_ref=dst,
        send_sem=send,
        recv_sem=recv,
        device_id={"ctx": peer},
        device_id_type=pl.DeviceIdType.MESH,
    )


def slice_kernel(
    query_hbm, key_hbm, value_hbm, cot_ref, weight_hbm, filt_ref,
    qback_ref, mback_ref, fgrad_ref,
    query_rows, key_rows, value_rows, weight_ref, mixed_ref, query_ref,
    mixed_in, query_in, cot_in, qgrad_ref, mgrad_ref, grad_ref, conv_ref, toep_ref, lag_ref,
    cot_send, cot_recv, mixed_send, mixed_recv, query_send, query_recv,
    qback_send, qback_recv, mback_send, mback_recv, local_sem,
):
    me = lax.axis_index("ctx")
    place_z, place_y, place_core = me // 4, (me // 2) % 2, me % 2
    y_peer = me + 2 - 4 * place_y
    core_peer = me + 1 - 2 * place_core

    def peer_of(step):
        return (me + step) % blocks

    loads = [
        pltpu.make_async_copy(src, dst, local_sem.at[6 + index])
        for index, (src, dst) in enumerate(
            [
                (key_hbm, key_rows),
                (value_hbm, value_rows),
                (query_hbm, query_rows),
                (weight_hbm, weight_ref),
            ]
        )
    ]
    for load in loads:
        load.start()

    barrier = pltpu.get_barrier_semaphore()

    @pl.loop(1, blocks)
    def _(step):
        pl.semaphore_signal(
            barrier, inc=1, device_id={"ctx": peer_of(step)}, device_id_type=pl.DeviceIdType.MESH
        )

    pl.semaphore_wait(barrier, blocks - 1)

    def cot_copy(src, block, way, peer):
        return remote(src, cot_in.at[block], cot_send.at[way, block], cot_recv.at[block], peer)

    def forward(src, block, ways, act):
        if "u" in ways:
            @pl.when(place_z < 3)
            def _():
                act(cot_copy(src, block, 0, me + 4))
        if "d" in ways:
            @pl.when(place_z > 0)
            def _():
                act(cot_copy(src, block, 1, me - 4))
        if "y" in ways:
            act(cot_copy(src, block, 2, y_peer))
        if "c" in ways:
            act(cot_copy(src, block, 3, core_peer))

    def arrived(block):
        cot_copy(cot_in.at[block], block, 3, core_peer).wait_recv()

    def begin(copy):
        copy.start()

    def sent(copy):
        copy.wait_send()

    def relay_z(hop, act, wait):
        @pl.when(place_z >= hop)
        def _():
            block = me - 4 * hop
            if wait:
                arrived(block)
            forward(cot_in.at[block], block, "uyc", act)

        @pl.when(place_z + hop <= 3)
        def _():
            block = me + 4 * hop
            if wait:
                arrived(block)
            forward(cot_in.at[block], block, "dyc", act)

    def relay_y(hop, act, wait):
        def one(block):
            if wait:
                arrived(block)
            forward(cot_in.at[block], block, "c", act)

        if hop == 0:
            one(y_peer)
        else:
            @pl.when(place_z >= hop)
            def _():
                one(y_peer - 4 * hop)

            @pl.when(place_z + hop <= 3)
            def _():
                one(y_peer + 4 * hop)

    def start_all(src, dst, send, recv, local, rows):
        pltpu.make_async_copy(src.at[me, rows], dst.at[me, rows], local).start()

        @pl.loop(1, blocks)
        def _(step):
            peer = peer_of(step)
            remote(src.at[peer, rows], dst.at[me, rows], send.at[peer], recv.at[me], peer).start()

    def wait_arrivals(src, dst, send, recv, local, rows):
        pltpu.make_async_copy(src.at[me, rows], dst.at[me, rows], local).wait()

        @pl.loop(1, blocks)
        def _(step):
            peer = peer_of(step)
            remote(
                src.at[peer, rows], dst.at[peer, rows], send.at[peer], recv.at[peer], peer
            ).wait_recv()

    def wait_sends(src, dst, send, recv, local, rows):
        @pl.loop(1, blocks)
        def _(step):
            peer = peer_of(step)
            remote(
                src.at[peer, rows], dst.at[me, rows], send.at[peer], recv.at[me], peer
            ).wait_send()

    every = pl.ds(0, mixed_in.shape[1])
    mixed_trip = (mixed_ref, mixed_in, mixed_send, mixed_recv, local_sem.at[0], every)
    query_trip = (query_ref, query_in, query_send, query_recv, local_sem.at[1], every)
    qback_trip = (qgrad_ref, qback_ref, qback_send, qback_recv, local_sem.at[2], every)
    halves = 2
    half_rows = mixed_in.shape[1] // halves
    mback_trips = [
        (
            mgrad_ref, mback_ref, mback_send.at[half], mback_recv.at[half],
            local_sem.at[4 + half], pl.ds(half * half_rows, half_rows),
        )
        for half in range(halves)
    ]

    def columns(dest):
        own = mixed_in.shape[1]
        return pl.ds(pl.multiple_of(dest * own, own), own)

    def grad_pair(block):
        other = block + 1 - 2 * place_core
        arrived(other)
        grad_block(block // 2, weight_ref, cot_in, grad_ref)

    def finish_block(dest):
        qgrad_ref[dest] = (
            conv_ref[dest] * grad_ref[dest].astype(jnp.float32)
        ).astype(jnp.bfloat16)

    def send_block(dest):
        finish_block(dest)
        remote(
            qgrad_ref.at[dest], qback_ref.at[me], qback_send.at[dest], qback_recv.at[me], dest
        ).start()

    def send_pair(block):
        send_block(block)
        send_block(block + 1 - 2 * place_core)

    def both_z(hop, base, act):
        @pl.when(place_z >= hop)
        def _():
            act(base - 4 * hop)

        @pl.when(place_z + hop <= 3)
        def _():
            act(base + 4 * hop)

    def grad_and_send(block):
        grad_pair(block)
        send_pair(block)

    forward(cot_ref, me, "udyc", begin)
    own_cot = pltpu.make_async_copy(cot_ref, cot_in.at[me], local_sem.at[3])
    own_cot.start()
    loads[0].wait()
    loads[1].wait()

    def make_mixed(dest):
        at = columns(dest)
        product = key_rows[:, at].astype(jnp.float32) * value_rows[:, at].astype(jnp.float32)
        mixed_ref[dest] = product.T.astype(jnp.bfloat16)

    @pl.loop(1, blocks)
    def _(step):
        peer = peer_of(step)
        make_mixed(peer)
        remote(
            mixed_ref.at[peer], mixed_in.at[me], mixed_send.at[peer], mixed_recv.at[me], peer
        ).start()

    make_mixed(me)
    pltpu.make_async_copy(mixed_ref.at[me, every], mixed_in.at[me, every], local_sem.at[0]).start()
    loads[2].wait()

    @pl.loop(0, blocks)
    def _(dest):
        query_ref[dest] = query_rows[:, columns(dest)].astype(jnp.float32).T.astype(jnp.bfloat16)

    @pl.loop(0, blocks)
    def _(group):
        toep_ref[group] = toeplitz(filt_ref[pl.ds(group, 1), :])

    own_cot.wait()
    loads[3].wait()
    relay_z(1, begin, True)
    relay_y(0, begin, True)
    grad_pair(me)
    relay_z(2, begin, True)
    relay_y(1, begin, True)
    start_all(*query_trip)
    both_z(1, me, grad_pair)
    grad_pair(y_peer)
    relay_z(3, begin, True)
    relay_y(2, begin, True)
    wait_arrivals(*mixed_trip)

    @pl.loop(0, blocks)
    def _(group):
        conv_group(group, mixed_in, toep_ref, conv_ref)

    finish_block(me)
    pltpu.make_async_copy(qgrad_ref.at[me, every], qback_ref.at[me, every], local_sem.at[2]).start()
    send_block(core_peer)
    both_z(1, me, send_pair)
    send_pair(y_peer)
    relay_y(3, begin, True)
    both_z(2, me, grad_and_send)
    both_z(1, y_peer, grad_and_send)
    both_z(3, me, grad_and_send)
    both_z(2, y_peer, grad_and_send)
    both_z(3, y_peer, grad_and_send)
    wait_arrivals(*query_trip)
    for half in range(halves):
        @pl.loop(half * blocks // halves, (half + 1) * blocks // halves)
        def _(group):
            corr_group(group, query_in, grad_ref, toep_ref, mgrad_ref)

        start_all(*mback_trips[half])

    @pl.loop(0, blocks)
    def _(group):
        lag_group(group, mixed_in, query_in, grad_ref, lag_ref)

    finish_lag(lag_ref, fgrad_ref)

    forward(cot_ref, me, "udyc", sent)
    for hop in (1, 2, 3):
        relay_z(hop, sent, False)
    for hop in (0, 1, 2, 3):
        relay_y(hop, sent, False)
    for trip in [mixed_trip, query_trip, qback_trip] + mback_trips:
        wait_sends(*trip)
    for trip in [qback_trip] + mback_trips:
        wait_arrivals(*trip)


def final_kernel(qgrad_ref, mgrad_ref, key_ref, value_ref, query_out, key_out, value_out):
    query_out[...] = qgrad_ref[...].astype(jnp.float32).T
    mgrad = mgrad_ref[...].astype(jnp.float32).T
    key_out[...] = mgrad * value_ref[...].astype(jnp.float32)
    value_out[...] = mgrad * key_ref[...].astype(jnp.float32)


def finish(qgrad, mgrad, key_proj, value_proj):
    chans = key_proj.shape[1]
    wide = chans // 4
    return pl.pallas_call(
        final_kernel,
        grid=(4,),
        in_specs=[pl.BlockSpec((wide, lane), lambda i: (i, 0))] * 2
        + [pl.BlockSpec((lane, wide), lambda i: (0, i))] * 2,
        out_specs=[pl.BlockSpec((lane, wide), lambda i: (0, i))] * 3,
        out_shape=[jax.ShapeDtypeStruct(key_proj.shape, jnp.float32)] * 3,
        compiler_params=pltpu.CompilerParams(vmem_limit_bytes=32 * 1024 * 1024),
        cost_estimate=pl.CostEstimate(flops=1 << 20, bytes_accessed=10 << 20, transcendentals=0),
    )(qgrad.reshape(chans, lane), mgrad.reshape(chans, lane), key_proj, value_proj)


def direct_device(query_proj, key_proj, value_proj, cotangent, out_weight, filters):
    own = out_weight.shape[0]
    features = cotangent.shape[1]
    seq_len = filters.shape[1]
    tile_shape = (blocks, own, lane)
    vmem = pl.BlockSpec(memory_space=pltpu.VMEM)
    anywhere = pl.BlockSpec(memory_space=pl.ANY)
    dma = pltpu.SemaphoreType.DMA
    tile = pltpu.VMEM(tile_shape, jnp.bfloat16)
    rows = pltpu.VMEM(query_proj.shape, jnp.bfloat16)
    qgrad, mgrad, filter_grad = pl.pallas_call(
        slice_kernel,
        in_specs=[anywhere] * 5 + [vmem],
        out_specs=[anywhere] * 2 + [vmem],
        out_shape=[
            jax.ShapeDtypeStruct(tile_shape, jnp.bfloat16),
            jax.ShapeDtypeStruct(tile_shape, jnp.bfloat16),
            jax.ShapeDtypeStruct(filters.shape, jnp.float32),
        ],
        scratch_shapes=[
            rows,
            rows,
            rows,
            pltpu.VMEM(out_weight.shape, jnp.bfloat16),
            tile,
            tile,
            tile,
            tile,
            pltpu.VMEM((blocks, lane, features), jnp.bfloat16),
            tile,
            tile,
            tile,
            pltpu.VMEM(tile_shape, jnp.float32),
            pltpu.VMEM((blocks, 2 * lane, seq_len), jnp.bfloat16),
            pltpu.VMEM((filters.shape[0], seq_len + lane), jnp.float32),
            dma((4, blocks)),
            dma((blocks,)),
            dma((blocks,)),
            dma((blocks,)),
            dma((blocks,)),
            dma((blocks,)),
            dma((blocks,)),
            dma((blocks,)),
            dma((2, blocks)),
            dma((2, blocks)),
            dma((10,)),
        ],
        compiler_params=pltpu.CompilerParams(
            collective_id=0, has_side_effects=True, vmem_limit_bytes=52 * 1024 * 1024
        ),
        cost_estimate=pl.CostEstimate(
            flops=8 << 30, bytes_accessed=16 << 20, transcendentals=0
        ),
    )(query_proj, key_proj, value_proj, cotangent, out_weight, filters)
    return (*finish(qgrad, mgrad, key_proj, value_proj), filter_grad)


def solution(mesh):
    placed = (
        P(("parts", "ctx"), None),
        P(("parts", "ctx"), None),
        P(("parts", "ctx"), None),
        P(("parts", "ctx"), None),
        P("ctx", None),
        P("ctx", None),
    )
    work = direct_device if mesh.shape["ctx"] == blocks else per_device
    return jax.shard_map(
        work,
        mesh=mesh,
        in_specs=placed,
        out_specs=(
            P(("parts", "ctx"), None),
            P(("parts", "ctx"), None),
            P(("parts", "ctx"), None),
            P(("parts", "ctx"), None),
        ),
        check_vma=False,
    )
```
